32 devices in a mesh: row: 8 (over y, x, core), col: 4 (over z).
Axes of the slice: x: 2, y: 2, z: 4, core: 2. Of those that a mesh axis runs over, the one named last changes fastest.
Arguments:
- phase: float32 [6, 32768], P(None, ('col', 'row')), may hold values from -6 to 6
- mass: float32 [32768], P(('col', 'row')), may hold values from 0.2 to 5
- active: int32 [256], P(('row', 'col')), may hold values from 0 to 32767, as said below
Outputs:
- accels: float32 [3, 256], P(None, ('row', 'col'))
- jerks: float32 [3, 256], P(None, ('row', 'col'))
The draws below stay inside these ranges and needn't reach their ends.
Inputs may be any that keep to these rules, and one draw needn't show every extreme that they name: `active`: the 256 indices are distinct.
All inputs are finite; a program needn't handle non-finite values.
Results may differ from the reference program's by a relative error of at most 0.0003.
Values sent between devices are 32-bit elements; how exact they have to be, the bound alone decides.
No kernel may reach another device: no remote copies, remote signals or barrier semaphores. Data moves between devices by JAX's collectives and lax.ppermute only.
A program may use at most 64 MiB of HBM per device.

```python
import math
import jax
import jax.numpy as jnp
from jax import lax

NSTARS = 32768
NACT = 256


def draw_active(key, part):
    first_key, second_key = jax.random.split(jax.random.fold_in(key, 11))
    others = 1 + jax.random.permutation(first_key, NSTARS - 2)[:NACT - 2]
    chosen = jnp.concatenate([jnp.array([0, NSTARS - 1], jnp.int32), others.astype(jnp.int32)])
    return jax.random.permutation(second_key, chosen)


def shard_levels(key, extent, cuts, low, largest):
    gain = 1.0
    for axis_at, blocks in cuts:
        draws = jax.random.uniform(jax.random.fold_in(jax.random.fold_in(key, 6), axis_at), (blocks,), jnp.float32, low / len(cuts), largest / len(cuts))
        gain = gain * jnp.repeat(jnp.exp(draws), extent[axis_at] // blocks).reshape((-1,) + (1,) * (len(extent) - 1 - axis_at))
    return gain


def normal_values(rng, shape, deviation, most, cuts=(), kind=jnp.bfloat16):
    values = jax.random.normal(rng, shape, jnp.float32) * deviation
    if len(cuts) > 0:
        values = shard_levels(rng, shape, cuts, -0.22, 0.18) * values
    return jnp.clip(values, min=-most, max=most).astype(kind)


def setup_inputs(seed: int = 0) -> dict:
    keys = jax.random.split(jax.random.key(seed), 4)
    phase = normal_values(keys[0], (6, NSTARS), 1.0, 6.0, ((1, 32),), jnp.float32)
    mass = jnp.clip(jnp.exp(math.log(5.0) - 3.218876 * jax.random.uniform(keys[1], (NSTARS,), jnp.float32) ** shard_levels(keys[1], (NSTARS,), ((0, 32),), -0.2, 0.2)), 0.2, 5.0)
    active = draw_active(jax.random.fold_in(keys[3], 71), 0)
    return dict(phase=phase, mass=mass, active=active)


SOFTENING = 0.0001

def pair_terms(targets, src_phase, src_mass):
    offset = src_phase[0:3, None, :] - targets[0:3, :, None]
    vel_diff = src_phase[3:6, None, :] - targets[3:6, :, None]
    dist_sq = lax.optimization_barrier(jnp.sum(offset * offset, axis=0)) + SOFTENING
    inverse = lax.rsqrt(dist_sq)
    inverse_sq = inverse * inverse
    weight = src_mass[None, :] * inverse * inverse_sq
    radial = 3.0 * lax.optimization_barrier(jnp.sum(offset * vel_diff, axis=0)) * inverse_sq
    accels = lax.optimization_barrier(jnp.sum(weight[None] * offset, axis=-1))
    jerks = lax.optimization_barrier(jnp.sum(weight[None] * (vel_diff - radial[None] * offset), axis=-1))
    return (accels, jerks)

def reference(phase, mass, active):
    targets = jnp.take(phase, active.astype(jnp.int32), axis=1)
    block_len = math.gcd(NSTARS, 512)
    block_count = NSTARS // block_len

    def add_block(carry, counter):
        first = (counter * block_len).astype(jnp.int32)
        src_phase = lax.dynamic_slice_in_dim(phase, first, block_len, 1)
        src_mass = lax.dynamic_slice_in_dim(mass, first, block_len, 0)
        accels, jerks = pair_terms(targets, src_phase, src_mass)
        return ((carry[0] + accels, carry[1] + jerks), None)
    zeros = jnp.zeros((3, NACT), jnp.float32)
    totals, unused = lax.scan(add_block, (zeros, zeros), jnp.arange(block_count, dtype=jnp.int32))
    return (totals[0] * (1.0 / NSTARS), totals[1] * (1.0 / NSTARS))
```

```python
import functools

import jax
import jax.numpy as jnp
from jax import lax
from jax.experimental import pallas as pl
from jax.experimental.pallas import tpu as pltpu
from jax.sharding import PartitionSpec as P

SOFTENING = 0.0001
LANES = 128


def pack_kernel(phase_ref, mass_ref, packed_ref):
    rows = packed_ref.shape[1]
    for part in range(6):
        for at in range(rows):
            packed_ref[part, at : at + 1, :] = phase_ref[part : part + 1, at * LANES : (at + 1) * LANES]
    packed_ref[6] = mass_ref[...]


def pack(phase, mass):
    rows = phase.shape[1] // LANES
    return pl.pallas_call(
        pack_kernel,
        out_shape=jax.ShapeDtypeStruct((7, rows, LANES), jnp.float32),
        in_specs=[pl.BlockSpec(memory_space=pltpu.VMEM)] * 2,
        out_specs=pl.BlockSpec(memory_space=pltpu.VMEM),
    )(phase, mass.reshape(rows, LANES))


def sweep_kernel(row_count, col_count, active_ref, stars_ref, accels_ref, jerks_ref):
    slots, _, rows, _ = stars_ref.shape
    count = active_ref.shape[0]
    col_at = lax.axis_index("col")
    lane = lax.broadcasted_iota(jnp.int32, (1, LANES), 1)
    picked = [[] for _ in range(6)]
    for target in range(count):
        star = active_ref[target]
        block = star // (rows * LANES)
        slot = (block % row_count) * col_count + ((block // row_count) ^ col_at)
        row = (star // LANES) % rows
        hit = lane == star % LANES
        for part in range(6):
            line = stars_ref[slot, part, pl.ds(row, 1), :]
            picked[part].append(jnp.where(hit, line, 0.0))
    targets = []
    for part in range(6):
        value = jnp.sum(jnp.concatenate(picked[part], axis=0), axis=1, keepdims=True)
        targets.append(jnp.broadcast_to(value, (count, LANES)))

    def add_slot(slot, sums):
        sums = list(sums)
        for row in range(rows):
            source = [
                jnp.broadcast_to(stars_ref[slot, part, row : row + 1, :], (count, LANES))
                for part in range(7)
            ]
            offset = [source[k] - targets[k] for k in range(3)]
            vel_diff = [source[k + 3] - targets[k + 3] for k in range(3)]
            dist_sq = offset[0] * offset[0] + offset[1] * offset[1] + offset[2] * offset[2] + SOFTENING
            along = offset[0] * vel_diff[0] + offset[1] * vel_diff[1] + offset[2] * vel_diff[2]
            inverse = lax.rsqrt(dist_sq)
            inverse_sq = inverse * inverse
            weight = source[6] * inverse * inverse_sq
            pull = weight * (along * inverse_sq)
            for k in range(3):
                sums[k] = sums[k] + weight * offset[k]
                sums[k + 3] = sums[k + 3] + weight * vel_diff[k]
                sums[k + 6] = sums[k + 6] + pull * offset[k]
        return tuple(sums)

    zeros = jnp.zeros((count, LANES), jnp.float32)
    sums = lax.fori_loop(0, slots, add_slot, (zeros,) * 9)
    norming = 1.0 / (slots * rows * LANES)
    out = zeros
    for k in range(6):
        total = sums[k] if k < 3 else sums[k] - 3.0 * sums[k + 3]
        out = jnp.where(lane == k, jnp.sum(total, axis=1, keepdims=True) * norming, out)
    out = out.T
    accels_ref[...] = out[0:3, :]
    jerks_ref[...] = out[3:6, :]


def sweep(active, stars, row_count, col_count):
    count = active.shape[0]
    return pl.pallas_call(
        functools.partial(sweep_kernel, row_count, col_count),
        out_shape=[jax.ShapeDtypeStruct((3, count), jnp.float32)] * 2,
        in_specs=[pl.BlockSpec(memory_space=pltpu.SMEM), pl.BlockSpec(memory_space=pltpu.VMEM)],
        out_specs=[pl.BlockSpec(memory_space=pltpu.VMEM)] * 2,
        compiler_params=pltpu.CompilerParams(vmem_limit_bytes=40 * 1024 * 1024),
    )(active, stars)


def shards(phase, mass, active):
    row_count = lax.axis_size("row")
    col_count = lax.axis_size("col")
    own = pack(phase, mass)
    blocks = [own]
    for step in range(1, col_count):
        blocks.append(lax.ppermute(own, "col", [(at, at ^ step) for at in range(col_count)]))
    stars = lax.all_gather(jnp.stack(blocks), "row", axis=0, tiled=True)
    return sweep(active, stars, row_count, col_count)


def solution(mesh):
    in_specs = (P(None, ("col", "row")), P(("col", "row")), P(("row", "col")))
    out_specs = (P(None, ("row", "col")), P(None, ("row", "col")))
    return jax.shard_map(shards, mesh=mesh, in_specs=in_specs, out_specs=out_specs, check_vma=False)
```

```python
import functools
import math

import jax
import jax.numpy as jnp
from jax import lax
from jax.experimental import pallas as pl
from jax.experimental.pallas import tpu as pltpu
from jax.sharding import PartitionSpec as P

SOFTENING = 0.0001
LANES = 128


def exchange_order(count):
    return sorted(range(1, count), key=lambda mask: (-mask.bit_length(), mask))


def swap(values, axis, mask):
    return lax.ppermute(values, axis, [(at, at ^ mask) for at in range(lax.axis_size(axis))])


def add_pairs(source, targets, sums):
    offset = [source[k] - targets[k] for k in range(3)]
    vel_diff = [source[k + 3] - targets[k + 3] for k in range(3)]
    dist_sq = offset[0] * offset[0] + offset[1] * offset[1] + offset[2] * offset[2] + SOFTENING
    along = offset[0] * vel_diff[0] + offset[1] * vel_diff[1] + offset[2] * vel_diff[2]
    inverse = lax.rsqrt(dist_sq)
    inverse_sq = inverse * inverse
    weight = source[6] * inverse * inverse_sq
    pull = weight * (along * inverse_sq)
    sums = list(sums)
    for k in range(3):
        sums[k] = sums[k] + weight * offset[k]
        sums[k + 3] = sums[k + 3] + weight * vel_diff[k]
        sums[k + 6] = sums[k + 6] + pull * offset[k]
    return tuple(sums)


def sweep_kernel(row_count, masks, active_ref, *refs):
    stacks, (accels_ref, jerks_ref) = refs[: len(masks)], refs[len(masks) :]
    slots, _, rows, _ = stacks[0].shape
    count = active_ref.shape[1]
    row_at, col_at = lax.axis_index("row"), lax.axis_index("col")
    lane = lax.broadcasted_iota(jnp.int32, (1, LANES), 1)
    place = lax.broadcasted_iota(jnp.int32, (1, count), 1)
    active = active_ref[...].astype(jnp.float32)
    picked = [[] for _ in range(6)]
    for target in range(count):
        star = jnp.sum(jnp.where(place == target, active, 0.0)).astype(jnp.int32)
        block = star // (rows * LANES)
        slot = (block // row_count) ^ col_at
        mask = (block % row_count) ^ row_at
        row = (star // LANES) % rows
        hit = lane == star % LANES
        for part in range(6):
            line = stacks[0][slot, part, pl.ds(row, 1), :]
            for at in range(1, len(masks)):
                line = jnp.where(mask == masks[at], stacks[at][slot, part, pl.ds(row, 1), :], line)
            picked[part].append(jnp.where(hit, line, 0.0))
    targets = []
    for part in range(6):
        value = jnp.sum(jnp.concatenate(picked[part], axis=0), axis=1, keepdims=True)
        targets.append(jnp.broadcast_to(value, (count, LANES)))

    zeros = jnp.zeros((count, LANES), jnp.float32)
    sums = (zeros,) * 9
    unroll = math.gcd(slots, 4)
    for stack in stacks:

        def add_slots(step, sums, stack=stack):
            for at in range(unroll):
                for row in range(rows):
                    source = [
                        jnp.broadcast_to(stack[step * unroll + at, part, row : row + 1, :], (count, LANES))
                        for part in range(7)
                    ]
                    sums = add_pairs(source, targets, sums)
            return sums

        sums = lax.fori_loop(0, slots // unroll, add_slots, sums)
    norming = 1.0 / (len(masks) * slots * rows * LANES)
    out = zeros
    for k in range(6):
        total = sums[k] if k < 3 else sums[k] - 3.0 * sums[k + 3]
        out = jnp.where(lane == k, jnp.sum(total, axis=1, keepdims=True) * norming, out)
    out = out.T
    accels_ref[...] = out[0:3, :]
    jerks_ref[...] = out[3:6, :]


def sweep(active, stacks, masks, row_count):
    count = active.shape[0]
    return pl.pallas_call(
        functools.partial(sweep_kernel, row_count, masks),
        out_shape=[jax.ShapeDtypeStruct((3, count), jnp.float32)] * 2,
        in_specs=[pl.BlockSpec(memory_space=pltpu.VMEM)] * (len(stacks) + 1),
        out_specs=[pl.BlockSpec(memory_space=pltpu.VMEM)] * 2,
        compiler_params=pltpu.CompilerParams(vmem_limit_bytes=40 * 1024 * 1024),
    )(active.reshape(1, count), *stacks)


def shards(phase, mass, active):
    row_count = lax.axis_size("row")
    col_count = lax.axis_size("col")
    rows = phase.shape[1] // LANES
    own = jnp.concatenate([phase.reshape(6, rows, LANES), mass.reshape(1, rows, LANES)], axis=0)
    stack = lax.dynamic_update_slice(jnp.zeros((col_count,) + own.shape, jnp.float32), own[None], (0, 0, 0, 0))
    for mask in exchange_order(col_count):
        stack = lax.dynamic_update_slice(stack, swap(own, "col", mask)[None], (mask, 0, 0, 0))
    stacks, masks = [], []
    for mask in [0] + [2 * mask for mask in reversed(exchange_order(row_count // 2))]:
        held = stack if mask == 0 else swap(stack, "row", mask)
        stacks += [held, swap(held, "row", 1)]
        masks += [mask, mask + 1]
    return sweep(active, stacks, masks, row_count)


def solution(mesh):
    in_specs = (P(None, ("col", "row")), P(("col", "row")), P(("row", "col")))
    out_specs = (P(None, ("row", "col")), P(None, ("row", "col")))
    return jax.shard_map(shards, mesh=mesh, in_specs=in_specs, out_specs=out_specs, check_vma=False)
```

```python
import functools

import jax
import jax.numpy as jnp
from jax import lax
from jax.experimental import pallas as pl
from jax.experimental.pallas import tpu as pltpu
from jax.sharding import PartitionSpec as P

SOFTENING = 0.0001
LANES = 128
PARTS = 7


def bit_reverse(value, count):
    out = 0
    for _ in range(count.bit_length() - 1):
        out = 2 * out + value % 2
        value = value // 2
    return out


def shift_order(count):
    return sorted(range(1, count), key=lambda shift: (min(shift, count - shift), shift))


def mask_order(count):
    return sorted(range(1, count), key=lambda mask: (-bin(mask).count("1"), mask))


def shift_cols(values, shift):
    count = lax.axis_size("col")
    pairs = [(at, bit_reverse((bit_reverse(at, count) + shift) % count, count)) for at in range(count)]
    return lax.ppermute(values, "col", pairs)


def swap_rows(values, mask):
    return lax.ppermute(values, "row", [(at, at ^ mask) for at in range(lax.axis_size("row"))])


def add_pairs(source, targets, sums):
    offset = [source[k] - targets[k] for k in range(3)]
    vel_diff = [source[k + 3] - targets[k + 3] for k in range(3)]
    dist_sq = offset[0] * offset[0] + offset[1] * offset[1] + offset[2] * offset[2] + SOFTENING
    along = offset[0] * vel_diff[0] + offset[1] * vel_diff[1] + offset[2] * vel_diff[2]
    inverse = lax.rsqrt(dist_sq)
    inverse_sq = inverse * inverse
    weight = source[6] * inverse * inverse_sq
    pull = weight * (along * inverse_sq)
    sums = list(sums)
    for k in range(3):
        sums[k] = sums[k] + weight * offset[k]
        sums[k + 3] = sums[k + 3] + weight * vel_diff[k]
        sums[k + 6] = sums[k + 6] + pull * offset[k]
    return tuple(sums)


def sweep_kernel(row_count, col_count, masks, active_ref, *refs):
    stacks, (accels_ref, jerks_ref) = refs[: len(masks)], refs[len(masks) :]
    rows = stacks[0].shape[0] // (PARTS * col_count)
    count = active_ref.shape[1]
    row_at = lax.axis_index("row")
    col_at = bit_reverse(lax.axis_index("col"), col_count)
    lane = lax.broadcasted_iota(jnp.int32, (count, LANES), 1)
    place = lax.broadcasted_iota(jnp.int32, (count, LANES), 0)
    zeros = jnp.zeros((count, LANES), jnp.float32)

    def lines(stack, first):
        return [
            jnp.broadcast_to(stack[pl.ds(first + part * rows, 1), :], (count, LANES)) for part in range(PARTS)
        ]

    picked = [[zeros, zeros] for _ in range(6)]
    for target in range(count):
        star = active_ref[0, target]
        block = star // (rows * LANES)
        slot = (col_at - bit_reverse(block // row_count, col_count) + col_count) % col_count
        mask = (block % row_count) ^ row_at
        first = slot * (PARTS * rows) + (star // LANES) % rows
        for at, stack in enumerate(stacks):
            hit = (lane == jnp.where(mask == masks[at], star % LANES, -1)) & (place == target)
            line = lines(stack, first)
            for part in range(6):
                picked[part][at % 2] = jnp.where(hit, line[part], picked[part][at % 2])
    targets = [
        jnp.broadcast_to(jnp.sum(one + other, axis=1, keepdims=True), (count, LANES)) for one, other in picked
    ]

    sums = (zeros,) * 9
    for stack in stacks:

        def add_slot(slot, sums, stack=stack):
            for row in range(rows):
                sums = add_pairs(lines(stack, slot * (PARTS * rows) + row), targets, sums)
            return sums

        sums = lax.fori_loop(0, col_count, add_slot, sums)
    norming = 1.0 / (row_count * col_count * rows * LANES)
    out = zeros
    for k in range(6):
        total = sums[k] if k < 3 else sums[k] - 3.0 * sums[k + 3]
        out = jnp.where(lane == k, jnp.sum(total, axis=1, keepdims=True) * norming, out)
    out = out.T
    accels_ref[...] = out[0:3, :]
    jerks_ref[...] = out[3:6, :]


def sweep(active, stacks, masks, row_count, col_count):
    count = active.shape[0]
    return pl.pallas_call(
        functools.partial(sweep_kernel, row_count, col_count, masks),
        out_shape=[jax.ShapeDtypeStruct((3, count), jnp.float32)] * 2,
        in_specs=[pl.BlockSpec(memory_space=pltpu.VMEM)] * (len(stacks) + 1),
        out_specs=[pl.BlockSpec(memory_space=pltpu.VMEM)] * 2,
        compiler_params=pltpu.CompilerParams(vmem_limit_bytes=40 * 1024 * 1024),
    )(active.reshape(1, count), *[stack.reshape(-1, LANES) for stack in stacks])


def shards(phase, mass, active):
    row_count = lax.axis_size("row")
    col_count = lax.axis_size("col")
    rows = phase.shape[1] // LANES
    own = jnp.concatenate([phase.reshape(6, rows, LANES), mass.reshape(1, rows, LANES)], axis=0)
    stack = lax.dynamic_update_slice(jnp.zeros((col_count,) + own.shape, jnp.float32), own[None], (0, 0, 0, 0))
    for shift in shift_order(col_count):
        stack = lax.dynamic_update_slice(stack, shift_cols(own, shift)[None], (shift, 0, 0, 0))
    stacks, masks = [], []
    for mask in [0] + [2 * mask for mask in reversed(mask_order(row_count // 2))]:
        held = stack if mask == 0 else swap_rows(stack, mask)
        stacks += [held, swap_rows(held, 1)]
        masks += [mask, mask + 1]
    return sweep(active, stacks, masks, row_count, col_count)


def solution(mesh):
    in_specs = (P(None, ("col", "row")), P(("col", "row")), P(("row", "col")))
    out_specs = (P(None, ("row", "col")), P(None, ("row", "col")))
    return jax.shard_map(shards, mesh=mesh, in_specs=in_specs, out_specs=out_specs, check_vma=False)
```

```python
import functools

import jax
import jax.numpy as jnp
from jax import lax
from jax.experimental import pallas as pl
from jax.experimental.pallas import tpu as pltpu
from jax.sharding import PartitionSpec as P

SOFTENING = 0.0001
LANES = 128
PARTS = 7


def bit_reverse(value, count):
    out = 0
    for _ in range(count.bit_length() - 1):
        out = 2 * out + value % 2
        value = value // 2
    return out


def shift_order(count):
    return sorted(range(1, count), key=lambda shift: (min(shift, count - shift), shift))


def mask_order(count):
    return sorted(range(1, count), key=lambda mask: (-bin(mask).count("1"), mask))


def shift_cols(values, shift):
    count = lax.axis_size("col")
    pairs = [(at, bit_reverse((bit_reverse(at, count) + shift) % count, count)) for at in range(count)]
    return lax.ppermute(values, "col", pairs)


def swap_rows(values, mask):
    return lax.ppermute(values, "row", [(at, at ^ mask) for at in range(lax.axis_size("row"))])


def add_pairs(source, targets, sums):
    offset = [source[k] - targets[k] for k in range(3)]
    vel_diff = [source[k + 3] - targets[k + 3] for k in range(3)]
    dist_sq = offset[0] * offset[0] + offset[1] * offset[1] + offset[2] * offset[2] + SOFTENING
    along = offset[0] * vel_diff[0] + offset[1] * vel_diff[1] + offset[2] * vel_diff[2]
    inverse = lax.rsqrt(dist_sq)
    inverse_sq = inverse * inverse
    weight = source[6] * inverse * inverse_sq
    pull = weight * (along * inverse_sq)
    sums = list(sums)
    for k in range(3):
        sums[k] = sums[k] + weight * offset[k]
        sums[k + 3] = sums[k + 3] + weight * vel_diff[k]
        sums[k + 6] = sums[k + 6] + pull * offset[k]
    return tuple(sums)


def sweep_kernel(row_count, col_count, masks, active_ref, *refs):
    stacks, (accels_ref, jerks_ref) = refs[: len(masks)], refs[len(masks) :]
    rows = stacks[0].shape[2]
    count = active_ref.shape[1]
    row_at = lax.axis_index("row")
    col_at = bit_reverse(lax.axis_index("col"), col_count)
    lane = lax.broadcasted_iota(jnp.int32, (count, LANES), 1)
    place = lax.broadcasted_iota(jnp.int32, (count, LANES), 0)
    zeros = jnp.zeros((count, LANES), jnp.float32)

    def lines(stack, slot, row):
        return [
            jnp.broadcast_to(stack[slot, part, pl.ds(row, 1), :], (count, LANES)) for part in range(PARTS)
        ]

    picked = [[zeros, zeros] for _ in range(6)]
    for target in range(count):
        star = active_ref[0, target]
        block = star // (rows * LANES)
        slot = (col_at - bit_reverse(block // row_count, col_count) + col_count) % col_count
        mask = (block % row_count) ^ row_at
        row = (star // LANES) % rows
        for at, stack in enumerate(stacks):
            hit = (lane == jnp.where(mask == masks[at], star % LANES, -1)) & (place == target)
            line = lines(stack, slot, row)
            for part in range(6):
                picked[part][at % 2] = jnp.where(hit, line[part], picked[part][at % 2])
    targets = [
        jnp.broadcast_to(jnp.sum(one + other, axis=1, keepdims=True), (count, LANES)) for one, other in picked
    ]

    sums = (zeros,) * 9
    for stack in stacks:

        def add_slot(slot, sums, stack=stack):
            for row in range(rows):
                sums = add_pairs(lines(stack, slot, row), targets, sums)
            return sums

        sums = lax.fori_loop(0, col_count, add_slot, sums)
    norming = 1.0 / (row_count * col_count * rows * LANES)
    out = zeros
    for k in range(6):
        total = sums[k] if k < 3 else sums[k] - 3.0 * sums[k + 3]
        out = jnp.where(lane == k, jnp.sum(total, axis=1, keepdims=True) * norming, out)
    out = out.T
    accels_ref[...] = out[0:3, :]
    jerks_ref[...] = out[3:6, :]


def sweep(active, stacks, masks, row_count, col_count):
    count = active.shape[0]
    return pl.pallas_call(
        functools.partial(sweep_kernel, row_count, col_count, masks),
        out_shape=[jax.ShapeDtypeStruct((3, count), jnp.float32)] * 2,
        in_specs=[pl.BlockSpec(memory_space=pltpu.VMEM)] * (len(stacks) + 1),
        out_specs=[pl.BlockSpec(memory_space=pltpu.VMEM)] * 2,
        compiler_params=pltpu.CompilerParams(vmem_limit_bytes=40 * 1024 * 1024),
    )(active.reshape(1, count), *stacks)


def shards(phase, mass, active):
    row_count = lax.axis_size("row")
    col_count = lax.axis_size("col")
    rows = phase.shape[1] // LANES
    own = jnp.concatenate([phase.reshape(6, rows, LANES), mass.reshape(1, rows, LANES)], axis=0)
    stack = lax.dynamic_update_slice(jnp.zeros((col_count,) + own.shape, jnp.float32), own[None], (0, 0, 0, 0))
    for shift in shift_order(col_count):
        stack = lax.dynamic_update_slice(stack, shift_cols(own, shift)[None], (shift, 0, 0, 0))
    stacks, masks = [], []
    for mask in [0] + [2 * mask for mask in reversed(mask_order(row_count // 2))]:
        held = stack if mask == 0 else swap_rows(stack, mask)
        stacks += [held, swap_rows(held, 1)]
        masks += [mask, mask + 1]
    return sweep(active, stacks, masks, row_count, col_count)


def solution(mesh):
    in_specs = (P(None, ("col", "row")), P(("col", "row")), P(("row", "col")))
    out_specs = (P(None, ("row", "col")), P(None, ("row", "col")))
    return jax.shard_map(shards, mesh=mesh, in_specs=in_specs, out_specs=out_specs, check_vma=False)
```

```python
import functools

import jax
import jax.numpy as jnp
from jax import lax
from jax.experimental import pallas as pl
from jax.experimental.pallas import tpu as pltpu
from jax.sharding import PartitionSpec as P

SOFTENING = 0.0001
LANES = 128
PARTS = 7


def split_index(value, size):
    if size & (size - 1) == 0:
        return value >> (size.bit_length() - 1), value & (size - 1)
    return lax.div(value, jnp.int32(size)), lax.rem(value, jnp.int32(size))


def mask_order(count):
    return sorted(range(1, count), key=lambda mask: (-bin(mask).count("1"), mask))


def swap_rows(values, mask):
    return lax.ppermute(values, "row", [(at, at ^ mask) for at in range(lax.axis_size("row"))])


def shift_cols(values, even, odd):
    rows, cols = lax.axis_size("row"), lax.axis_size("col")
    pairs = []
    for row in range(rows):
        for col in range(cols):
            to = (col + (odd if row % 2 else even)) % cols
            pairs.append((row * cols + col, row * cols + to))
    return lax.ppermute(values, ("row", "col"), pairs)


def put(values, block, at):
    return lax.dynamic_update_slice(values, block, (at, 0, 0, 0))


def gather_cols(own):
    cols = lax.axis_size("col")
    stack = put(jnp.zeros((cols,) + own.shape, jnp.float32), own[None], 0)
    pair = put(jnp.zeros((2,) + own.shape, jnp.float32), own[None], 0)
    pair = put(pair, swap_rows(own, 1)[None], 1)
    if cols > 1:
        stack = put(stack, shift_cols(own, 1, 1)[None], 1)
    for shift in range(2, cols, 2):
        stack = put(stack, shift_cols(pair, shift, shift + 1), shift)
    return stack


def locate(star, rows, row_count, col_count):
    block, inside = split_index(star, rows * LANES)
    line, lane = split_index(inside, LANES)
    col, row = split_index(block, row_count)
    back = split_index(lax.axis_index("col") - col + col_count, col_count)[1]
    far = back >= 2
    holder = jnp.where(far, (row & -2) | (back & 1), row)
    slot = jnp.where(far, (back & -2) + jnp.where(holder == row, 0, 1), back)
    return holder ^ lax.axis_index("row"), slot, line, lane


def add_pairs(source, targets, sums):
    offset = [source[k] - targets[k] for k in range(3)]
    vel_diff = [source[k + 3] - targets[k + 3] for k in range(3)]
    dist_sq = offset[0] * offset[0] + offset[1] * offset[1] + offset[2] * offset[2] + SOFTENING
    along = offset[0] * vel_diff[0] + offset[1] * vel_diff[1] + offset[2] * vel_diff[2]
    inverse = lax.rsqrt(dist_sq)
    inverse_sq = inverse * inverse
    weight = source[6] * inverse * inverse_sq
    pull = weight * (along * inverse_sq)
    sums = list(sums)
    for k in range(3):
        sums[k] = sums[k] + weight * offset[k]
        sums[k + 3] = sums[k + 3] + weight * vel_diff[k]
        sums[k + 6] = sums[k + 6] + pull * offset[k]
    return tuple(sums)


def sweep_kernel(row_count, col_count, masks, active_ref, *refs):
    stacks, (accels_ref, jerks_ref) = refs[: len(masks)], refs[len(masks) :]
    rows = stacks[0].shape[2]
    count = active_ref.shape[1]
    lane = lax.broadcasted_iota(jnp.int32, (count, LANES), 1)
    place = lax.broadcasted_iota(jnp.int32, (count, LANES), 0)
    zeros = jnp.zeros((count, LANES), jnp.float32)

    def lines(stack, slot, row):
        return [
            jnp.broadcast_to(stack[slot, part, pl.ds(row, 1), :], (count, LANES)) for part in range(PARTS)
        ]

    picked = [[zeros, zeros] for _ in range(6)]
    for target in range(count):
        mask, slot, row, spot = locate(active_ref[0, target], rows, row_count, col_count)
        for at, stack in enumerate(stacks):
            hit = (lane == jnp.where(mask == masks[at], spot, -1)) & (place == target)
            line = lines(stack, slot, row)
            for part in range(6):
                picked[part][at % 2] = jnp.where(hit, line[part], picked[part][at % 2])
    targets = [
        jnp.broadcast_to(jnp.sum(one + other, axis=1, keepdims=True), (count, LANES)) for one, other in picked
    ]

    sums = (zeros,) * 9
    for stack in stacks:

        def add_slot(slot, sums, stack=stack):
            for row in range(rows):
                sums = add_pairs(lines(stack, slot, row), targets, sums)
            return sums

        sums = lax.fori_loop(0, col_count, add_slot, sums)
    norming = 1.0 / (row_count * col_count * rows * LANES)
    out = zeros
    for k in range(6):
        total = sums[k] if k < 3 else sums[k] - 3.0 * sums[k + 3]
        out = jnp.where(lane == k, jnp.sum(total, axis=1, keepdims=True) * norming, out)
    out = out.T
    accels_ref[...] = out[0:3, :]
    jerks_ref[...] = out[3:6, :]


def sweep(active, stacks, masks, row_count, col_count):
    count = active.shape[0]
    return pl.pallas_call(
        functools.partial(sweep_kernel, row_count, col_count, masks),
        out_shape=[jax.ShapeDtypeStruct((3, count), jnp.float32)] * 2,
        in_specs=[pl.BlockSpec(memory_space=pltpu.VMEM)] * (len(stacks) + 1),
        out_specs=[pl.BlockSpec(memory_space=pltpu.VMEM)] * 2,
        compiler_params=pltpu.CompilerParams(vmem_limit_bytes=40 * 1024 * 1024),
    )(active.reshape(1, count), *stacks)


def shards(phase, mass, active):
    row_count = lax.axis_size("row")
    col_count = lax.axis_size("col")
    rows = phase.shape[1] // LANES
    own = jnp.concatenate([phase.reshape(6, rows, LANES), mass.reshape(1, rows, LANES)], axis=0)
    stack = gather_cols(own)
    stacks, masks = [], []
    for mask in [0] + [2 * mask for mask in reversed(mask_order(row_count // 2))]:
        held = stack if mask == 0 else swap_rows(stack, mask)
        stacks += [held, swap_rows(held, 1)]
        masks += [mask, mask + 1]
    return sweep(active, stacks, masks, row_count, col_count)


def solution(mesh):
    in_specs = (P(None, ("col", "row")), P(("col", "row")), P(("row", "col")))
    out_specs = (P(None, ("row", "col")), P(None, ("row", "col")))
    return jax.shard_map(shards, mesh=mesh, in_specs=in_specs, out_specs=out_specs, check_vma=False)
```

```python
import functools
import math

import jax
import jax.numpy as jnp
from jax import lax
from jax.experimental import pallas as pl
from jax.experimental.pallas import tpu as pltpu
from jax.sharding import PartitionSpec as P

SOFTENING = 0.0001
LANES = 128
PARTS = 7


def split_index(value, size):
    if size & (size - 1) == 0:
        return value >> (size.bit_length() - 1), value & (size - 1)
    return lax.div(value, jnp.int32(size)), lax.rem(value, jnp.int32(size))


def mask_order(count):
    return sorted(range(1, count), key=lambda mask: (-bin(mask).count("1"), mask))


def swap_rows(values, mask):
    return lax.ppermute(values, "row", [(at, at ^ mask) for at in range(lax.axis_size("row"))])


def shift_cols(values, even, odd):
    rows, cols = lax.axis_size("row"), lax.axis_size("col")
    pairs = []
    for row in range(rows):
        for col in range(cols):
            to = (col + (odd if row % 2 else even)) % cols
            pairs.append((row * cols + col, row * cols + to))
    return lax.ppermute(values, ("row", "col"), pairs)


def put(values, block, at):
    return lax.dynamic_update_slice(values, block, (at, 0, 0, 0))


def gather_cols(own):
    cols = lax.axis_size("col")
    stack = put(jnp.zeros((cols,) + own.shape, jnp.float32), own[None], 0)
    pair = put(jnp.zeros((2,) + own.shape, jnp.float32), own[None], 0)
    pair = put(pair, swap_rows(own, 1)[None], 1)
    if cols > 1:
        stack = put(stack, shift_cols(own, 1, 1)[None], 1)
    for shift in range(2, cols, 2):
        stack = put(stack, shift_cols(pair, shift, shift + 1), shift)
    return stack


def locate(star, rows, row_count, col_count):
    block, inside = split_index(star, rows * LANES)
    line, lane = split_index(inside, LANES)
    col, row = split_index(block, row_count)
    back = split_index(lax.axis_index("col") - col + col_count, col_count)[1]
    far = back >= 2
    holder = jnp.where(far, (row & -2) | (back & 1), row)
    slot = jnp.where(far, (back & -2) + jnp.where(holder == row, 0, 1), back)
    return holder ^ lax.axis_index("row"), slot, line, lane


def add_pairs(source, targets, sums):
    offset = [source[k] - targets[k] for k in range(3)]
    vel_diff = [source[k + 3] - targets[k + 3] for k in range(3)]
    dist_sq = offset[0] * offset[0] + offset[1] * offset[1] + offset[2] * offset[2] + SOFTENING
    along = offset[0] * vel_diff[0] + offset[1] * vel_diff[1] + offset[2] * vel_diff[2]
    inverse = lax.rsqrt(dist_sq)
    inverse_sq = inverse * inverse
    weight = source[6] * inverse * inverse_sq
    along = along * inverse_sq
    sums = list(sums)
    for k in range(3):
        pull = weight * offset[k]
        sums[k] = sums[k] + pull
        sums[k + 3] = sums[k + 3] + weight * vel_diff[k]
        sums[k + 6] = sums[k + 6] + along * pull
    return tuple(sums)


def sweep_kernel(row_count, col_count, masks, active_ref, *refs):
    stacks, (accels_ref, jerks_ref) = refs[: len(masks)], refs[len(masks) :]
    rows = stacks[0].shape[2]
    count = active_ref.shape[1]
    lane = lax.broadcasted_iota(jnp.int32, (count, LANES), 1)
    place = lax.broadcasted_iota(jnp.int32, (count, LANES), 0)
    zeros = jnp.zeros((count, LANES), jnp.float32)

    def lines(stack, slot, row):
        return [
            jnp.broadcast_to(stack[slot, part, pl.ds(row, 1), :], (count, LANES)) for part in range(PARTS)
        ]

    picked = [zeros] * 6
    for target in range(count):
        mask, slot, row, spot = locate(active_ref[0, target], rows, row_count, col_count)
        for at, stack in enumerate(stacks):
            hit = (lane == jnp.where(mask == masks[at], spot, -1)) & (place == target)
            line = lines(stack, slot, row)
            picked = [jnp.where(hit, line[part], picked[part]) for part in range(6)]
    targets = [jnp.broadcast_to(jnp.sum(value, axis=1, keepdims=True), (count, LANES)) for value in picked]

    sums = (zeros,) * 9
    unroll = math.gcd(col_count, 2)
    for stack in stacks:

        def add_slots(step, sums, stack=stack):
            for at in range(unroll):
                for row in range(rows):
                    sums = add_pairs(lines(stack, step * unroll + at, row), targets, sums)
            return sums

        sums = lax.fori_loop(0, col_count // unroll, add_slots, sums)
    norming = 1.0 / (row_count * col_count * rows * LANES)
    out = zeros
    for k in range(6):
        total = sums[k] if k < 3 else sums[k] - 3.0 * sums[k + 3]
        out = jnp.where(lane == k, jnp.sum(total, axis=1, keepdims=True) * norming, out)
    out = out.T
    accels_ref[...] = out[0:3, :]
    jerks_ref[...] = out[3:6, :]


def sweep(active, stacks, masks, row_count, col_count):
    count = active.shape[0]
    return pl.pallas_call(
        functools.partial(sweep_kernel, row_count, col_count, masks),
        out_shape=[jax.ShapeDtypeStruct((3, count), jnp.float32)] * 2,
        in_specs=[pl.BlockSpec(memory_space=pltpu.VMEM)] * (len(stacks) + 1),
        out_specs=[pl.BlockSpec(memory_space=pltpu.VMEM)] * 2,
        compiler_params=pltpu.CompilerParams(vmem_limit_bytes=40 * 1024 * 1024),
    )(active.reshape(1, count), *stacks)


def shards(phase, mass, active):
    row_count = lax.axis_size("row")
    col_count = lax.axis_size("col")
    rows = phase.shape[1] // LANES
    own = jnp.concatenate([phase.reshape(6, rows, LANES), mass.reshape(1, rows, LANES)], axis=0)
    stack = gather_cols(own)
    stacks, masks = [], []
    for mask in [0] + [2 * mask for mask in reversed(mask_order(row_count // 2))]:
        held = stack if mask == 0 else swap_rows(stack, mask)
        stacks += [held, swap_rows(held, 1)]
        masks += [mask, mask + 1]
    return sweep(active, stacks, masks, row_count, col_count)


def solution(mesh):
    in_specs = (P(None, ("col", "row")), P(("col", "row")), P(("row", "col")))
    out_specs = (P(None, ("row", "col")), P(None, ("row", "col")))
    return jax.shard_map(shards, mesh=mesh, in_specs=in_specs, out_specs=out_specs, check_vma=False)
```

```python
import functools

import jax
import jax.numpy as jnp
from jax import lax
from jax.experimental import pallas as pl
from jax.experimental.pallas import tpu as pltpu
from jax.sharding import PartitionSpec as P

SOFTENING = 0.0001
LANES = 128
PARTS = 7


def split_index(value, size):
    if size & (size - 1) == 0:
        return value >> (size.bit_length() - 1), value & (size - 1)
    return lax.div(value, jnp.int32(size)), lax.rem(value, jnp.int32(size))


def mask_order(count):
    return sorted(range(1, count), key=lambda mask: (-bin(mask).count("1"), mask))


def swap_rows(values, mask):
    return lax.ppermute(values, "row", [(at, at ^ mask) for at in range(lax.axis_size("row"))])


def shift_cols(values, even, odd):
    rows, cols = lax.axis_size("row"), lax.axis_size("col")
    pairs = []
    for row in range(rows):
        for col in range(cols):
            to = (col + (odd if row % 2 else even)) % cols
            pairs.append((row * cols + col, row * cols + to))
    return lax.ppermute(values, ("row", "col"), pairs)


def put(values, block, at):
    return lax.dynamic_update_slice(values, block, (at, 0, 0, 0))


def gather_cols(own):
    cols = lax.axis_size("col")
    stack = put(jnp.zeros((cols,) + own.shape, jnp.float32), own[None], 0)
    pair = put(jnp.zeros((2,) + own.shape, jnp.float32), own[None], 0)
    pair = put(pair, swap_rows(own, 1)[None], 1)
    if cols > 1:
        stack = put(stack, shift_cols(own, 1, 1)[None], 1)
    for shift in range(2, cols, 2):
        stack = put(stack, shift_cols(pair, shift, shift + 1), shift)
    return stack


def locate(star, rows, row_count, col_count):
    block, inside = split_index(star, rows * LANES)
    line, lane = split_index(inside, LANES)
    col, row = split_index(block, row_count)
    back = split_index(lax.axis_index("col") - col + col_count, col_count)[1]
    far = back >= 2
    holder = jnp.where(far, (row & -2) | (back & 1), row)
    slot = jnp.where(far, (back & -2) + jnp.where(holder == row, 0, 1), back)
    return holder ^ lax.axis_index("row"), slot, line, lane


def add_pairs(source, targets, sums):
    offset = [source[k] - targets[k] for k in range(3)]
    vel_diff = [source[k + 3] - targets[k + 3] for k in range(3)]
    dist_sq = offset[0] * offset[0] + offset[1] * offset[1] + offset[2] * offset[2] + SOFTENING
    along = offset[0] * vel_diff[0] + offset[1] * vel_diff[1] + offset[2] * vel_diff[2]
    inverse = lax.rsqrt(dist_sq)
    inverse_sq = inverse * inverse
    weight = source[6] * inverse * inverse_sq
    along = along * inverse_sq
    sums = list(sums)
    for k in range(3):
        pull = weight * offset[k]
        sums[k] = sums[k] + pull
        sums[k + 3] = sums[k + 3] + weight * vel_diff[k]
        sums[k + 6] = sums[k + 6] + along * pull
    return tuple(sums)


def sweep_kernel(row_count, col_count, masks, active_ref, *refs):
    stacks, (accels_ref, jerks_ref) = refs[: len(masks)], refs[len(masks) :]
    rows = stacks[0].shape[2]
    count = active_ref.shape[1]
    lane = lax.broadcasted_iota(jnp.int32, (count, LANES), 1)
    place = lax.broadcasted_iota(jnp.int32, (count, LANES), 0)
    zeros = jnp.zeros((count, LANES), jnp.float32)

    def lines(stack, slot, row):
        return [
            jnp.broadcast_to(stack[slot, part, pl.ds(row, 1), :], (count, LANES)) for part in range(PARTS)
        ]

    picked = [zeros] * 6
    for target in range(count):
        mask, slot, row, spot = locate(active_ref[0, target], rows, row_count, col_count)
        for at, stack in enumerate(stacks):
            hit = (lane == jnp.where(mask == masks[at], spot, -1)) & (place == target)
            line = lines(stack, slot, row)
            picked = [jnp.where(hit, line[part], picked[part]) for part in range(6)]
    targets = [jnp.broadcast_to(jnp.sum(value, axis=1, keepdims=True), (count, LANES)) for value in picked]

    def add_slot(slot, sums):
        for stack in stacks:
            for row in range(rows):
                sums = add_pairs(lines(stack, slot, row), targets, sums)
        return sums

    sums = lax.fori_loop(0, col_count, add_slot, (zeros,) * 9)
    norming = 1.0 / (row_count * col_count * rows * LANES)
    for k in range(6):
        total = sums[k] if k < 3 else sums[k] - 3.0 * sums[k + 3]
        total = jnp.sum(total, axis=1, keepdims=True) * norming
        total = jnp.sum(jnp.where(lane == place, total, 0.0), axis=0, keepdims=True)[:, 0:count]
        if k < 3:
            accels_ref[k : k + 1, :] = total
        else:
            jerks_ref[k - 3 : k - 2, :] = total


def sweep(active, stacks, masks, row_count, col_count):
    count = active.shape[0]
    return pl.pallas_call(
        functools.partial(sweep_kernel, row_count, col_count, masks),
        out_shape=[jax.ShapeDtypeStruct((3, count), jnp.float32)] * 2,
        in_specs=[pl.BlockSpec(memory_space=pltpu.VMEM)] * (len(stacks) + 1),
        out_specs=[pl.BlockSpec(memory_space=pltpu.VMEM)] * 2,
        compiler_params=pltpu.CompilerParams(vmem_limit_bytes=40 * 1024 * 1024),
    )(active.reshape(1, count), *stacks)


def shards(phase, mass, active):
    row_count = lax.axis_size("row")
    col_count = lax.axis_size("col")
    rows = phase.shape[1] // LANES
    own = jnp.concatenate([phase.reshape(6, rows, LANES), mass.reshape(1, rows, LANES)], axis=0)
    stack = gather_cols(own)
    stacks, masks = [], []
    for mask in [0] + [2 * mask for mask in reversed(mask_order(row_count // 2))]:
        held = stack if mask == 0 else swap_rows(stack, mask)
        stacks += [held, swap_rows(held, 1)]
        masks += [mask, mask + 1]
    return sweep(active, stacks, masks, row_count, col_count)


def solution(mesh):
    in_specs = (P(None, ("col", "row")), P(("col", "row")), P(("row", "col")))
    out_specs = (P(None, ("row", "col")), P(None, ("row", "col")))
    return jax.shard_map(shards, mesh=mesh, in_specs=in_specs, out_specs=out_specs, check_vma=False)
```

```python
import functools

import jax
import jax.numpy as jnp
from jax import lax
from jax.experimental import pallas as pl
from jax.experimental.pallas import tpu as pltpu
from jax.sharding import PartitionSpec as P

SOFTENING = 0.0001
LANES = 128
PARTS = 7


def split_index(value, size):
    if size & (size - 1) == 0:
        return value >> (size.bit_length() - 1), value & (size - 1)
    return lax.div(value, jnp.int32(size)), lax.rem(value, jnp.int32(size))


def ring_place(chip):
    for shift in (1, 2, 4):
        chip = chip ^ (chip >> shift)
    return chip


def shift_order(count):
    return sorted(range(1, count), key=lambda shift: (min(shift, count - shift), shift))


def shift_chips(values, shift):
    rows = lax.axis_size("row")
    pairs = []
    for row in range(rows):
        place = (ring_place(row // 2) + shift) % (rows // 2)
        pairs.append((row, 2 * (place ^ (place >> 1)) + row % 2))
    return lax.ppermute(values, "row", pairs)


def swap_rows(values, mask):
    return lax.ppermute(values, "row", [(at, at ^ mask) for at in range(lax.axis_size("row"))])


def shift_cols(values, even, odd):
    rows, cols = lax.axis_size("row"), lax.axis_size("col")
    pairs = []
    for row in range(rows):
        for col in range(cols):
            to = (col + (odd if row % 2 else even)) % cols
            pairs.append((row * cols + col, row * cols + to))
    return lax.ppermute(values, ("row", "col"), pairs)


def put(values, block, at):
    return lax.dynamic_update_slice(values, block, (at, 0, 0, 0))


def gather_cols(own):
    cols = lax.axis_size("col")
    stack = put(jnp.zeros((cols,) + own.shape, jnp.float32), own[None], 0)
    pair = put(jnp.zeros((2,) + own.shape, jnp.float32), own[None], 0)
    pair = put(pair, swap_rows(own, 1)[None], 1)
    if cols > 1:
        stack = put(stack, shift_cols(own, 1, 1)[None], 1)
    for shift in range(2, cols, 2):
        stack = put(stack, shift_cols(pair, shift, shift + 1), shift)
    return stack


def locate(star, rows, row_count, col_count):
    block, inside = split_index(star, rows * LANES)
    line, lane = split_index(inside, LANES)
    col, row = split_index(block, row_count)
    back = split_index(lax.axis_index("col") - col + col_count, col_count)[1]
    far = back >= 2
    holder = jnp.where(far, (row & -2) | (back & 1), row)
    slot = jnp.where(far, (back & -2) + jnp.where(holder == row, 0, 1), back)
    row_at = lax.axis_index("row")
    shift = ring_place(row_at >> 1) - ring_place(holder >> 1) + row_count // 2
    shift = split_index(shift, row_count // 2)[1]
    return 2 * shift + ((holder ^ row_at) & 1), slot, line, lane


def add_pairs(source, targets, sums):
    offset = [source[k] - targets[k] for k in range(3)]
    vel_diff = [source[k + 3] - targets[k + 3] for k in range(3)]
    dist_sq = offset[0] * offset[0] + offset[1] * offset[1] + offset[2] * offset[2] + SOFTENING
    along = offset[0] * vel_diff[0] + offset[1] * vel_diff[1] + offset[2] * vel_diff[2]
    inverse = lax.rsqrt(dist_sq)
    inverse_sq = inverse * inverse
    weight = source[6] * inverse * inverse_sq
    along = along * inverse_sq
    sums = list(sums)
    for k in range(3):
        pull = weight * offset[k]
        sums[k] = sums[k] + pull
        sums[k + 3] = sums[k + 3] + weight * vel_diff[k]
        sums[k + 6] = sums[k + 6] + along * pull
    return tuple(sums)


def sweep_kernel(row_count, col_count, labels, active_ref, *refs):
    stacks, (accels_ref, jerks_ref) = refs[: len(labels)], refs[len(labels) :]
    rows = stacks[0].shape[2]
    count = active_ref.shape[1]
    lane = lax.broadcasted_iota(jnp.int32, (count, LANES), 1)
    place = lax.broadcasted_iota(jnp.int32, (count, LANES), 0)
    zeros = jnp.zeros((count, LANES), jnp.float32)

    def lines(stack, slot, row):
        return [
            jnp.broadcast_to(stack[slot, part, pl.ds(row, 1), :], (count, LANES)) for part in range(PARTS)
        ]

    picked = [zeros] * 6
    for target in range(count):
        label, slot, row, spot = locate(active_ref[0, target], rows, row_count, col_count)
        for at, stack in enumerate(stacks):
            hit = (lane == jnp.where(label == labels[at], spot, -1)) & (place == target)
            line = lines(stack, slot, row)
            picked = [jnp.where(hit, line[part], picked[part]) for part in range(6)]
    targets = [jnp.broadcast_to(jnp.sum(value, axis=1, keepdims=True), (count, LANES)) for value in picked]

    def add_slot(slot, sums):
        for stack in stacks:
            for row in range(rows):
                sums = add_pairs(lines(stack, slot, row), targets, sums)
        return sums

    sums = lax.fori_loop(0, col_count, add_slot, (zeros,) * 9)
    norming = 1.0 / (row_count * col_count * rows * LANES)
    for k in range(6):
        total = sums[k] if k < 3 else sums[k] - 3.0 * sums[k + 3]
        total = jnp.sum(total, axis=1, keepdims=True) * norming
        total = jnp.sum(jnp.where(lane == place, total, 0.0), axis=0, keepdims=True)[:, 0:count]
        if k < 3:
            accels_ref[k : k + 1, :] = total
        else:
            jerks_ref[k - 3 : k - 2, :] = total


def sweep(active, stacks, labels, row_count, col_count):
    count = active.shape[0]
    return pl.pallas_call(
        functools.partial(sweep_kernel, row_count, col_count, labels),
        out_shape=[jax.ShapeDtypeStruct((3, count), jnp.float32)] * 2,
        in_specs=[pl.BlockSpec(memory_space=pltpu.VMEM)] * (len(stacks) + 1),
        out_specs=[pl.BlockSpec(memory_space=pltpu.VMEM)] * 2,
        compiler_params=pltpu.CompilerParams(vmem_limit_bytes=40 * 1024 * 1024),
    )(active.reshape(1, count), *stacks)


def shards(phase, mass, active):
    row_count = lax.axis_size("row")
    col_count = lax.axis_size("col")
    rows = phase.shape[1] // LANES
    own = jnp.concatenate([phase.reshape(6, rows, LANES), mass.reshape(1, rows, LANES)], axis=0)
    stack = gather_cols(own)
    stacks, labels = [], []
    for shift in [0] + shift_order(row_count // 2)[::-1]:
        held = stack if shift == 0 else shift_chips(stack, shift)
        stacks += [held, swap_rows(held, 1)]
        labels += [2 * shift, 2 * shift + 1]
    return sweep(active, stacks, labels, row_count, col_count)


def solution(mesh):
    in_specs = (P(None, ("col", "row")), P(("col", "row")), P(("row", "col")))
    out_specs = (P(None, ("row", "col")), P(None, ("row", "col")))
    return jax.shard_map(shards, mesh=mesh, in_specs=in_specs, out_specs=out_specs, check_vma=False)
```

```python
import functools

import jax
import jax.numpy as jnp
from jax import lax
from jax.experimental import pallas as pl
from jax.experimental.pallas import tpu as pltpu
from jax.sharding import PartitionSpec as P

SOFTENING = 0.0001
LANES = 128
PARTS = 7


def split_index(value, size):
    if size & (size - 1) == 0:
        return value >> (size.bit_length() - 1), value & (size - 1)
    return lax.div(value, jnp.int32(size)), lax.rem(value, jnp.int32(size))


def ring_place(chip):
    for shift in (1, 2, 4):
        chip = chip ^ (chip >> shift)
    return chip


def shift_order(count):
    return sorted(range(1, count), key=lambda shift: (min(shift, count - shift), shift))


def shift_chips(values, shift):
    rows = lax.axis_size("row")
    pairs = []
    for row in range(rows):
        place = (ring_place(row // 2) + shift) % (rows // 2)
        pairs.append((row, 2 * (place ^ (place >> 1)) + row % 2))
    return lax.ppermute(values, "row", pairs)


def swap_rows(values, mask):
    return lax.ppermute(values, "row", [(at, at ^ mask) for at in range(lax.axis_size("row"))])


def shift_cols(values, even, odd):
    rows, cols = lax.axis_size("row"), lax.axis_size("col")
    pairs = []
    for row in range(rows):
        for col in range(cols):
            to = (col + (odd if row % 2 else even)) % cols
            pairs.append((row * cols + col, row * cols + to))
    return lax.ppermute(values, ("row", "col"), pairs)


def put(values, block, at):
    return lax.dynamic_update_slice(values, block, (at, 0, 0, 0))


def gather_cols(own):
    cols = lax.axis_size("col")
    stack = put(jnp.zeros((cols,) + own.shape, jnp.float32), own[None], 0)
    pair = put(jnp.zeros((2,) + own.shape, jnp.float32), own[None], 0)
    pair = put(pair, swap_rows(own, 1)[None], 1)
    if cols > 1:
        stack = put(stack, shift_cols(own, 1, 1)[None], 1)
    for shift in range(2, cols, 2):
        stack = put(stack, shift_cols(pair, shift, shift + 1), shift)
    return stack


def locate(star, rows, row_count, col_count):
    block, inside = split_index(star, rows * LANES)
    line, lane = split_index(inside, LANES)
    col, row = split_index(block, row_count)
    back = split_index(lax.axis_index("col") - col + col_count, col_count)[1]
    far = back >= 2
    holder = jnp.where(far, (row & -2) | (back & 1), row)
    slot = jnp.where(far, (back & -2) + jnp.where(holder == row, 0, 1), back)
    row_at = lax.axis_index("row")
    shift = ring_place(row_at >> 1) - ring_place(holder >> 1) + row_count // 2
    shift = split_index(shift, row_count // 2)[1]
    return 2 * shift + ((holder ^ row_at) & 1), slot, line, lane


def add_pairs(source, targets, sums):
    offset = [source[k] - targets[k] for k in range(3)]
    vel_diff = [source[k + 3] - targets[k + 3] for k in range(3)]
    dist_sq = offset[0] * offset[0] + offset[1] * offset[1] + offset[2] * offset[2] + SOFTENING
    along = offset[0] * vel_diff[0] + offset[1] * vel_diff[1] + offset[2] * vel_diff[2]
    inverse = lax.rsqrt(dist_sq)
    inverse_sq = inverse * inverse
    weight = source[6] * inverse * inverse_sq
    along = along * inverse_sq
    sums = list(sums)
    for k in range(3):
        pull = weight * offset[k]
        sums[k] = sums[k] + pull
        sums[k + 3] = sums[k + 3] + weight * vel_diff[k]
        sums[k + 6] = sums[k + 6] + along * pull
    return tuple(sums)


def sweep_kernel(row_count, col_count, labels, active_ref, *refs):
    stacks, (accels_ref, jerks_ref) = refs[: len(labels)], refs[len(labels) :]
    rows = stacks[0].shape[2]
    count = active_ref.shape[1]
    lane = lax.broadcasted_iota(jnp.int32, (count, LANES), 1)
    place = lax.broadcasted_iota(jnp.int32, (count, LANES), 0)
    zeros = jnp.zeros((count, LANES), jnp.float32)

    def lines(stack, slot, row):
        return [
            jnp.broadcast_to(stack[slot, part, pl.ds(row, 1), :], (count, LANES)) for part in range(PARTS)
        ]

    picked = [zeros] * 6
    for target in range(count):
        label, slot, row, spot = locate(active_ref[0, target], rows, row_count, col_count)
        for at, stack in enumerate(stacks):
            hit = (lane == jnp.where(label == labels[at], spot, -1)) & (place == target)
            line = lines(stack, slot, row)
            picked = [jnp.where(hit, line[part], picked[part]) for part in range(6)]
    targets = [jnp.broadcast_to(jnp.sum(value, axis=1, keepdims=True), (count, LANES)) for value in picked]

    def add_slot(slot, sums):
        for stack in stacks:
            for row in range(rows):
                sums = add_pairs(lines(stack, slot, row), targets, sums)
        return sums

    sums = lax.fori_loop(0, col_count, add_slot, (zeros,) * 9)
    norming = 1.0 / (row_count * col_count * rows * LANES)
    for k in range(6):
        total = sums[k] if k < 3 else sums[k] - 3.0 * sums[k + 3]
        total = jnp.sum(total, axis=1, keepdims=True) * norming
        total = jnp.sum(jnp.where(lane == place, total, 0.0), axis=0, keepdims=True)[:, 0:count]
        if k < 3:
            accels_ref[k : k + 1, :] = total
        else:
            jerks_ref[k - 3 : k - 2, :] = total


def sweep(active, stacks, labels, row_count, col_count):
    count = active.shape[0]
    return pl.pallas_call(
        functools.partial(sweep_kernel, row_count, col_count, labels),
        out_shape=[jax.ShapeDtypeStruct((3, count), jnp.float32)] * 2,
        in_specs=[pl.BlockSpec(memory_space=pltpu.VMEM)] * (len(stacks) + 1),
        out_specs=[pl.BlockSpec(memory_space=pltpu.VMEM)] * 2,
        compiler_params=pltpu.CompilerParams(vmem_limit_bytes=40 * 1024 * 1024),
    )(active.reshape(1, count), *stacks)


def shards(phase, mass, active):
    row_count = lax.axis_size("row")
    col_count = lax.axis_size("col")
    rows = phase.shape[1] // LANES
    own = jnp.concatenate([phase.reshape(6, rows, LANES), mass.reshape(1, rows, LANES)], axis=0)
    stack = gather_cols(own)
    stacks, labels = [stack], [0]
    for shift in shift_order(row_count // 2)[::-1]:
        held = shift_chips(stack, shift)
        stacks += [held, swap_rows(held, 1)]
        labels += [2 * shift, 2 * shift + 1]
    stacks.append(swap_rows(stack, 1))
    labels.append(1)
    return sweep(active, stacks, labels, row_count, col_count)


def solution(mesh):
    in_specs = (P(None, ("col", "row")), P(("col", "row")), P(("row", "col")))
    out_specs = (P(None, ("row", "col")), P(None, ("row", "col")))
    return jax.shard_map(shards, mesh=mesh, in_specs=in_specs, out_specs=out_specs, check_vma=False)
```

```python
import functools

import jax
import jax.numpy as jnp
from jax import lax
from jax.experimental import pallas as pl
from jax.experimental.pallas import tpu as pltpu
from jax.sharding import PartitionSpec as P

SOFTENING = 0.0001
LANES = 128
PARTS = 7


def split_index(value, size):
    if size & (size - 1) == 0:
        return value >> (size.bit_length() - 1), value & (size - 1)
    return lax.div(value, jnp.int32(size)), lax.rem(value, jnp.int32(size))


def ring_place(chip):
    for shift in (1, 2, 4):
        chip = chip ^ (chip >> shift)
    return chip


def shift_order(count):
    return sorted(range(1, count), key=lambda shift: (-min(shift, count - shift), -shift))


def shift_chips(values, shift):
    rows = lax.axis_size("row")
    pairs = []
    for row in range(rows):
        place = (ring_place(row // 2) + shift) % (rows // 2)
        pairs.append((row, 2 * (place ^ (place >> 1)) + row % 2))
    return lax.ppermute(values, "row", pairs)


def swap_rows(values, mask):
    return lax.ppermute(values, "row", [(at, at ^ mask) for at in range(lax.axis_size("row"))])


def shift_cols(values, even, odd):
    rows, cols = lax.axis_size("row"), lax.axis_size("col")
    pairs = []
    for row in range(rows):
        for col in range(cols):
            to = (col + (odd if row % 2 else even)) % cols
            pairs.append((row * cols + col, row * cols + to))
    return lax.ppermute(values, ("row", "col"), pairs)


def put(values, block, at):
    return lax.dynamic_update_slice(values, block, (at, 0, 0, 0))


def gather_cols(own):
    cols = lax.axis_size("col")
    stack = put(jnp.zeros((cols,) + own.shape, jnp.float32), own[None], 0)
    pair = put(jnp.zeros((2,) + own.shape, jnp.float32), own[None], 0)
    pair = put(pair, swap_rows(own, 1)[None], 1)
    if cols > 1:
        stack = put(stack, shift_cols(own, 1, 1)[None], 1)
    for shift in range(2, cols, 2):
        stack = put(stack, shift_cols(pair, shift, shift + 1), shift)
    return stack


def locate(star, rows, row_count, col_count):
    block, inside = split_index(star, rows * LANES)
    line, lane = split_index(inside, LANES)
    col, row = split_index(block, row_count)
    back = split_index(lax.axis_index("col") - col + col_count, col_count)[1]
    far = back >= 2
    holder = jnp.where(far, (row & -2) | (back & 1), row)
    slot = jnp.where(far, (back & -2) + jnp.where(holder == row, 0, 1), back)
    row_at = lax.axis_index("row")
    shift = ring_place(row_at >> 1) - ring_place(holder >> 1) + row_count // 2
    shift = split_index(shift, row_count // 2)[1]
    return 2 * shift + ((holder ^ row_at) & 1), slot, line, lane


def add_pairs(source, targets, sums):
    offset = [source[k] - targets[k] for k in range(3)]
    vel_diff = [source[k + 3] - targets[k + 3] for k in range(3)]
    dist_sq = offset[0] * offset[0] + offset[1] * offset[1] + offset[2] * offset[2] + SOFTENING
    along = offset[0] * vel_diff[0] + offset[1] * vel_diff[1] + offset[2] * vel_diff[2]
    inverse = lax.rsqrt(dist_sq)
    inverse_sq = inverse * inverse
    weight = source[6] * inverse * inverse_sq
    along = along * inverse_sq
    sums = list(sums)
    for k in range(3):
        pull = weight * offset[k]
        sums[k] = sums[k] + pull
        sums[k + 3] = sums[k + 3] + weight * vel_diff[k]
        sums[k + 6] = sums[k + 6] + along * pull
    return tuple(sums)


def sweep_kernel(row_count, col_count, labels, active_ref, *refs):
    stacks, (accels_ref, jerks_ref) = refs[: len(labels)], refs[len(labels) :]
    rows = stacks[0].shape[2]
    count = active_ref.shape[1]
    lane = lax.broadcasted_iota(jnp.int32, (count, LANES), 1)
    place = lax.broadcasted_iota(jnp.int32, (count, LANES), 0)
    zeros = jnp.zeros((count, LANES), jnp.float32)

    def lines(stack, slot, row):
        return [
            jnp.broadcast_to(stack[slot, part, pl.ds(row, 1), :], (count, LANES)) for part in range(PARTS)
        ]

    picked = [zeros] * 6
    for target in range(count):
        label, slot, row, spot = locate(active_ref[0, target], rows, row_count, col_count)
        for at, stack in enumerate(stacks):
            hit = (lane == jnp.where(label == labels[at], spot, -1)) & (place == target)
            line = lines(stack, slot, row)
            picked = [jnp.where(hit, line[part], picked[part]) for part in range(6)]
    targets = [jnp.broadcast_to(jnp.sum(value, axis=1, keepdims=True), (count, LANES)) for value in picked]

    def add_slot(slot, sums):
        for stack in stacks:
            for row in range(rows):
                sums = add_pairs(lines(stack, slot, row), targets, sums)
        return sums

    sums = lax.fori_loop(0, col_count, add_slot, (zeros,) * 9)
    norming = 1.0 / (row_count * col_count * rows * LANES)
    for k in range(6):
        total = sums[k] if k < 3 else sums[k] - 3.0 * sums[k + 3]
        total = jnp.sum(total, axis=1, keepdims=True) * norming
        total = jnp.sum(jnp.where(lane == place, total, 0.0), axis=0, keepdims=True)[:, 0:count]
        if k < 3:
            accels_ref[k : k + 1, :] = total
        else:
            jerks_ref[k - 3 : k - 2, :] = total


def sweep(active, stacks, labels, row_count, col_count):
    count = active.shape[0]
    return pl.pallas_call(
        functools.partial(sweep_kernel, row_count, col_count, labels),
        out_shape=[jax.ShapeDtypeStruct((3, count), jnp.float32)] * 2,
        in_specs=[pl.BlockSpec(memory_space=pltpu.VMEM)] * (len(stacks) + 1),
        out_specs=[pl.BlockSpec(memory_space=pltpu.VMEM)] * 2,
        compiler_params=pltpu.CompilerParams(vmem_limit_bytes=40 * 1024 * 1024),
    )(active.reshape(1, count), *stacks)


def shards(phase, mass, active):
    row_count = lax.axis_size("row")
    col_count = lax.axis_size("col")
    rows = phase.shape[1] // LANES
    own = jnp.concatenate([phase.reshape(6, rows, LANES), mass.reshape(1, rows, LANES)], axis=0)
    stack = gather_cols(own)
    stacks, labels = [], []
    for shift in [0] + shift_order(row_count // 2)[::-1]:
        held = stack if shift == 0 else shift_chips(stack, shift)
        stacks += [held, swap_rows(held, 1)]
        labels += [2 * shift, 2 * shift + 1]
    return sweep(active, stacks, labels, row_count, col_count)


def solution(mesh):
    in_specs = (P(None, ("col", "row")), P(("col", "row")), P(("row", "col")))
    out_specs = (P(None, ("row", "col")), P(None, ("row", "col")))
    return jax.shard_map(shards, mesh=mesh, in_specs=in_specs, out_specs=out_specs, check_vma=False)
```
